128 devices in a mesh: band: 8 (over z_lo, y), fft: 16 (over x, z_hi, core).
Axes of the slice: x: 4, y: 4, z: 4 (z_hi: 2, z_lo: 2; z = z_hi * 2 + z_lo), core: 2. Of those that a mesh axis runs over, the one named last changes fastest.
Arguments:
- orbitals: float32 [8, 256, 256, 256], P('band', 'fft'), may hold values from -6 to 6
- pair_flags: int32 [8, 2], replicated, may hold values 0 or 1
- cutoff_reach: int32 [129, 129], replicated, may hold values from 0 to 128
Outputs:
- exchange_field: float32 [8, 256, 256, 256], P('band', 'fft')
- margin: float32 [8, 1], P('band')
The draws below stay inside these ranges and needn't reach their ends.
All inputs are finite; a program needn't handle non-finite values.
Results may differ from the reference program's by a relative error of at most 0.0003.
Values sent between devices are 32-bit elements; how exact they have to be, the bound alone decides.
A program may use at most 128 MiB of HBM per device.

```python
import jax
import jax.numpy as jnp
from jax import lax

NG = 256
B_DEV = 1
NBANDS = 8
HALF = 129
N_BAND = 8


def place_ends(result, stream_key, least, high):
    shape = result.shape
    spot = [jax.random.randint(jax.random.fold_in(stream_key, axis), (), 0, shape[axis]) for axis in range(len(shape))]
    result = result.at[tuple(spot)].set(least)
    longest = shape.index(max(shape))
    spot[longest] = (spot[longest] + 1) % shape[longest]
    return result.at[tuple(spot)].set(high)


def levels(own_key, extent, cuts, least, largest):
    loudness, own = 1.0, jax.random.fold_in(own_key, 6)
    for axis_at, parts in cuts:
        heights = jnp.exp(jax.random.uniform(jax.random.fold_in(own, axis_at), (parts,), jnp.float32, least / len(cuts), largest / len(cuts)))
        loudness = loudness * jnp.repeat(heights, extent[axis_at] // parts).reshape([-1 if axis == axis_at else 1 for axis in range(len(extent))])
    return loudness


def centred(key, shape, spread, reach, cuts=(), held_as=jnp.bfloat16):
    entries = jax.random.normal(key, shape, jnp.float32) * spread
    if len(cuts) > 0:
        entries = levels(key, shape, cuts, -0.22, 0.18) * entries
    return jnp.clip(entries, min=-reach, max=reach).astype(held_as)


def setup_inputs(seed: int = 0) -> dict:
    key_of = jax.random.split(jax.random.key(seed), 4)
    return {
        "orbitals": centred(key_of[0], (NBANDS, NG, NG, NG), 1.0, 6.0, ((0, 8), (1, 16)), jnp.float32),
        "pair_flags": place_ends((jax.random.randint(key_of[1], (N_BAND, 2), 0, 4) < 3).astype(jnp.int32), jax.random.fold_in(key_of[1], 1), 0, 1),
        "cutoff_reach": place_ends(jax.random.randint(key_of[2], (HALF, HALF), 0, HALF), jax.random.fold_in(key_of[2], 1), 0, HALF - 1).astype(jnp.int32),
    }


def folded(count):
    indices = jnp.arange(count, dtype=jnp.int32)
    return jnp.minimum(indices, count - indices).astype(jnp.int32)


def coulomb_table(cutoff_reach):
    fold_all = folded(NG)
    reach_map = cutoff_reach[fold_all][:, fold_all]
    inside = fold_all[None, None, :] <= reach_map[:, :, None]
    squares = (fold_all[:, None, None] * fold_all[:, None, None]
               + fold_all[None, :, None] * fold_all[None, :, None]
               + fold_all[None, None, :] * fold_all[None, None, :])
    safe_sq = jnp.maximum(squares, 1).astype(jnp.float32)
    return jnp.where(inside & (squares > 0), 64.0 / safe_sq, 0.0).astype(jnp.float32)


def potential(density, kernel):
    spectrum = jnp.fft.fftn(density)
    return jnp.real(jnp.fft.ifftn(kernel * spectrum)).astype(jnp.float32)


def reference(orbitals, pair_flags, cutoff_reach):
    kernel = coulomb_table(cutoff_reach)
    weights = pair_flags.astype(jnp.float32)
    band_total = orbitals.shape[0]
    applied = [jnp.zeros(orbitals.shape[1:], jnp.float32) for _ in range(band_total)]
    for slice_id in range(N_BAND):
        first_row = slice_id * B_DEV
        next_first = ((slice_id + 1) % N_BAND) * B_DEV
        for a in range(B_DEV):
            for b in range(a, B_DEV):
                i = first_row + a
                j = first_row + b
                coulomb = potential(weights[slice_id, 0] * orbitals[i] * orbitals[j], kernel)
                applied[i] = applied[i] - orbitals[j] * coulomb
                if i != j:
                    applied[j] = applied[j] - orbitals[i] * coulomb
            for b in range(B_DEV):
                i = first_row + a
                j = next_first + b
                coulomb = potential(weights[slice_id, 1] * orbitals[i] * orbitals[j], kernel)
                applied[i] = applied[i] - orbitals[j] * coulomb
                applied[j] = applied[j] - orbitals[i] * coulomb
    exchange_field = jnp.stack(applied)
    margin_rows = []
    for slice_id in range(N_BAND):
        first_row = slice_id * B_DEV
        own_orbitals = orbitals[first_row:first_row + B_DEV]
        own_applied = exchange_field[first_row:first_row + B_DEV]
        block = jnp.einsum('axyz,bxyz->ab', own_orbitals, own_applied, precision=lax.Precision.HIGHEST)
        margin_rows.append(block / float(NG * NG))
    margin = jnp.concatenate(margin_rows, axis=0)
    return exchange_field, margin
```

```python
import functools
import math

import jax
import jax.numpy as jnp
import ml_dtypes
import numpy as np
from jax import lax
from jax.experimental import pallas as pl
from jax.experimental.pallas import tpu as pltpu
from jax.sharding import PartitionSpec as P

MESH = pl.DeviceIdType.MESH
N = 256
PLANES = 16
HALF = 129
BANDS = 8
GROUP = 16
PARTS = 4
W = 128

STEPS = (
    (2, 1, 0), (1, 0, 0), (3, 0, 1), (0, 1, 0), (2, 0, 0), (1, 1, 1), (3, 1, 0), (0, 1, 1),
    (2, 1, 1), (3, 0, 0), (1, 0, 1), (0, 0, 1), (2, 0, 1), (3, 1, 1), (1, 1, 0),
)


def cas_tables():
    steps = np.arange(N)
    angles = (steps[:, None] * steps[None, :] % N) * (2.0 * math.pi / N)
    table = np.cos(angles) + np.sin(angles)
    terms = []
    for _ in range(3):
        terms.append(table.astype(ml_dtypes.bfloat16))
        table = table - terms[-1].astype(np.float64)
    order = [terms[i] for i in (0, 1, 0, 1, 2, 0)]
    return np.concatenate(order, axis=0), np.concatenate(order, axis=1)


def split(x, axis, passes):
    high = x.astype(jnp.bfloat16)
    rest = x - high.astype(jnp.float32)
    middle = rest.astype(jnp.bfloat16)
    terms = [high, high, middle]
    if passes == 6:
        low = (rest - middle.astype(jnp.float32)).astype(jnp.bfloat16)
        terms = terms + [middle, high, low]
    return jnp.concatenate(terms, axis=axis)


def kernel(
    orb_hbm, flags, reach, tall, wide, out_hbm, margin,
    orb, fol, a0, a1, s0, s1, b0, b1, hin, acc, ktab, part, parts, fol_pass, hand_pass,
    load_sem, fol_send, fol_recv, fwd_send, fwd_recv, back_send, back_recv,
    hand_send, hand_recv, out_sem, sum_send, sum_recv, pass_send, pass_recv,
):
    band = lax.axis_index("band")
    me = lax.axis_index("fft")
    row = lax.rem(band, 4)
    across = 4 - 4 * (band // 4)
    after = lax.rem(band + 1, BANDS)
    before = lax.rem(band + BANDS - 1, BANDS)

    def partner(step):
        x, z, core = me // 4, (me // 2) % 2, me % 2
        return ((x + step[0]) % 4) * 4 + ((z + step[1]) % 2) * 2 + (core + step[2]) % 2

    def send(source, target, send_sem, recv_sem, device):
        pltpu.make_async_remote_copy(
            src_ref=source, dst_ref=target, send_sem=send_sem, recv_sem=recv_sem,
            device_id=device, device_id_type=MESH,
        ).start()

    def await_bytes(ref, sem):
        pltpu.make_async_copy(ref, ref, sem).wait()

    def right(x, passes):
        return jnp.dot(split(x, 1, passes), tall[: passes * N], preferred_element_type=jnp.float32)

    def left(x, passes):
        return jnp.dot(wide[:, : passes * N], split(x, 0, passes), preferred_element_type=jnp.float32)

    def put(ref, index, x):
        for h in range(2):
            ref[h, index] = x[:, h * W:(h + 1) * W]

    def line(ref, index):
        halves = [ref.at[h].reshape(N * PLANES, W)[pl.ds(index, N, stride=PLANES), :] for h in range(2)]
        return jnp.concatenate(halves, axis=1)

    loads = [
        pltpu.make_async_copy(
            orb_hbm.at[0, pl.ds(c * PARTS, PARTS)], orb.at[pl.ds(c * PARTS, PARTS)], load_sem.at[c]
        )
        for c in range(PARTS)
    ]
    for load in loads:
        load.start()

    barrier = pltpu.get_barrier_semaphore()
    for step in STEPS:
        pl.semaphore_signal(barrier, inc=1, device_id=(band, partner(step)), device_id_type=MESH)
    for ahead in range(1, BANDS):
        other = lax.rem(band + ahead, BANDS)
        pl.semaphore_signal(barrier, inc=1, device_id=(other, me), device_id_type=MESH)
    pl.semaphore_wait(barrier, GROUP - 1 + BANDS - 1)

    own_weight = flags[band, 0].astype(jnp.float32)
    next_weight = flags[band, 1].astype(jnp.float32)

    for c in range(PARTS):
        loads[c].wait()

    @pl.when(row != 0)
    def _():
        for c in range(PARTS):
            rows = pl.ds(c * PARTS, PARTS)
            send(orb.at[rows], fol.at[rows], fol_send, fol_recv.at[c], (before, me))

    @pl.when(row == 0)
    def _():
        for c in range(PARTS):
            rows = pl.ds(c * PARTS, PARTS)
            if c == 3:
                send(orb.at[rows], fol.at[rows], fol_send, fol_recv.at[c], (across + 3, me))
            else:
                send(orb.at[rows], fol_pass, fol_send, pass_recv.at[0], (across + c, me))

    def pass_following():
        @pl.when(row != 3)
        def _():
            await_bytes(fol_pass, pass_recv.at[0])
            rows = pl.ds(row * PARTS, PARTS)
            send(fol_pass, fol.at[rows], pass_send.at[0], fol_recv.at[row], (band - row + 3, me))

    def forward(c, pair, weight, spectrum, lines, which):
        for q in range(PARTS):
            p = c * PARTS + q
            density = weight * orb[p] * pair[p]
            put(spectrum, p, left(right(density, 6), 6))
        rows = pl.ds(c * PARTS, PARTS)
        mine = pl.ds(me * PLANES + c * PARTS, PARTS)
        for step in STEPS:
            g = partner(step)
            send(
                spectrum.at[:, rows, pl.ds(pl.multiple_of(g * PLANES, PLANES), PLANES)],
                lines.at[:, mine], fwd_send.at[which], fwd_recv.at[which], (band, g),
            )
        pltpu.make_async_copy(
            spectrum.at[:, rows, pl.ds(pl.multiple_of(me * PLANES, PLANES), PLANES)],
            lines.at[:, mine], fwd_recv.at[which],
        ).start()

    def own_chunk(c, carry):
        forward(c, orb, own_weight, a0, s0, 0)
        return carry

    lax.fori_loop(0, PARTS, own_chunk, 0)

    def fold(shape, axis):
        k = lax.broadcasted_iota(jnp.int32, shape, axis)
        return jnp.minimum(k, N - k)

    level = lax.broadcasted_iota(jnp.int32, (N, N), 1)
    pick_x = (fold((N, N), 0) == level).astype(jnp.bfloat16)
    by_x = jnp.dot(pick_x, reach[...], preferred_element_type=jnp.float32).astype(jnp.bfloat16)

    def table_step(k, carry):
        ky = me * PLANES + k
        fold_y = jnp.minimum(ky, N - ky)
        pick_y = (lax.broadcasted_iota(jnp.int32, (N, N), 0) == fold_y).astype(jnp.bfloat16)
        limit = jnp.dot(by_x, pick_y, preferred_element_type=jnp.float32)
        fold_x, fold_z = fold((N, N), 0), fold((N, N), 1)
        squares = fold_x * fold_x + fold_z * fold_z + fold_y * fold_y
        kept = (fold_z.astype(jnp.float32) <= limit) & (squares > 0)
        value = (64.0 / N**3) / jnp.maximum(squares, 1).astype(jnp.float32)
        ktab[k] = jnp.where(kept, value, 0.0)
        return carry

    lax.fori_loop(0, PLANES, table_step, 0)

    def cross_chunk(c, carry):
        await_bytes(fol.at[pl.ds(0, PARTS)], fol_recv.at[c])
        forward(c, fol, next_weight, a1, s1, 1)
        return carry

    def middle(lines, restored, which):
        await_bytes(lines, fwd_recv.at[which])
        await_bytes(restored.at[:, pl.ds(0, GROUP - 1)], fwd_send.at[which])

        def one(k):
            put(restored, k, left(left(line(lines, k), 6) * ktab[k], 3))

        def pair(i, carry):
            one(2 * i)
            one(2 * i + 1)
            return carry

        lax.fori_loop(0, PLANES // 2, pair, 0)

    def send_back(restored, mixed, which, j):
        mine = pl.ds(pl.multiple_of(me * PLANES, PLANES), PLANES)
        half = pl.ds(8 * j, 8)
        for step in STEPS:
            g = partner(step)
            send(
                restored.at[:, :, pl.ds(pl.multiple_of(g * PLANES + 8 * j, 8), 8)],
                mixed.at[:, mine, half], back_send.at[which], back_recv.at[which, j], (band, g),
            )
        pltpu.make_async_copy(
            restored.at[:, :, pl.ds(pl.multiple_of(me * PLANES + 8 * j, 8), 8)],
            mixed.at[:, mine, half], back_recv.at[which, j],
        ).start()

    pass_following()
    lax.fori_loop(0, PARTS // 2, cross_chunk, 0)
    middle(s0, a0, 0)
    send_back(a0, b0, 0, 0)
    send_back(a0, b0, 0, 1)
    lax.fori_loop(PARTS // 2, PARTS, cross_chunk, 0)
    middle(s1, a1, 1)
    send_back(a1, b1, 1, 0)
    send_back(a1, b1, 1, 1)

    def potential(mixed, p):
        return right(left(line(mixed, p), 3), 3)

    def hand(j):
        @pl.when(row != 3)
        def _():
            for c in (2 * j, 2 * j + 1):
                rows = pl.ds(PARTS * PLANES * c, PARTS * PLANES)
                send(s0.at[:, rows], hin.at[:, rows], hand_send, hand_recv.at[c], (after, me))

        @pl.when(row == 3)
        def _():
            for c in (2 * j, 2 * j + 1):
                rows = pl.ds(PARTS * PLANES * c, PARTS * PLANES)
                if c == 0:
                    send(s0.at[:, rows], hin.at[:, rows], hand_send, hand_recv.at[c], (across, me))
                else:
                    send(s0.at[:, rows], hand_pass, hand_send, pass_recv.at[1], (across + c, me))

    def pass_handed():
        @pl.when(row != 0)
        def _():
            await_bytes(hand_pass, pass_recv.at[1])
            rows = pl.ds(PARTS * PLANES * row, PARTS * PLANES)
            send(hand_pass, hin.at[:, rows], pass_send.at[1], hand_recv.at[row], (band - row, me))

    for j in range(2):
        await_bytes(b1.at[:, :, pl.ds(8 * j, 8)], back_recv.at[1, j])

        def cross_out(i, carry, j=j):
            for q in range(2):
                p = 8 * j + 2 * i + q
                coulomb = potential(b1, p)
                acc[p] = fol[p] * coulomb
                handed = orb[p] * coulomb
                for h in range(2):
                    s0[h, pl.ds(p * PLANES, PLANES)] = handed[:, h * W:(h + 1) * W].reshape(PLANES, PLANES, W)
            return carry

        lax.fori_loop(0, 4, cross_out, 0)
        hand(j)

    for j in range(2):
        await_bytes(b0.at[:, :, pl.ds(8 * j, 8)], back_recv.at[0, j])

        def own_out(i, carry, j=j):
            for q in range(2):
                p = 8 * j + 2 * i + q
                acc[p] = acc[p] + orb[p] * potential(b0, p)
            return carry

        lax.fori_loop(0, 4, own_out, 0)

    pass_handed()

    part[...] = jnp.zeros_like(part)
    for c in range(PARTS):
        await_bytes(hin.at[:, pl.ds(0, PARTS * PLANES)], hand_recv.at[c])

        def finish(i, carry, c=c):
            p = PARTS * c + i
            given = [hin[h, pl.ds(p * PLANES, PLANES)].reshape(N, W) for h in range(2)]
            field = -(acc[p] + jnp.concatenate(given, axis=1))
            acc[p] = field
            sums = (orb[p] * field).reshape(N // 8, 8, N).sum(axis=0)
            part[...] += sums[:, :W] + sums[:, W:]
            return carry

        lax.fori_loop(0, PARTS, finish, 0)
        rows = pl.ds(PARTS * c, PARTS)
        pltpu.make_async_copy(acc.at[rows], out_hbm.at[0, rows], out_sem.at[c]).start()

    for step in STEPS:
        send(part, parts.at[me], sum_send, sum_recv, (band, partner(step)))
    pltpu.make_async_copy(part, parts.at[me], sum_recv).start()
    await_bytes(parts, sum_recv)
    total = jnp.sum(jnp.sum(parts[...], axis=0), keepdims=True)
    margin[...] = total / float(N * N)

    await_bytes(parts.at[pl.ds(0, GROUP - 1)], sum_send)
    await_bytes(fol, fol_send)
    await_bytes(hin, hand_send)
    for which, restored in enumerate((a0, a1)):
        await_bytes(restored.at[:, pl.ds(0, GROUP - 1)], back_send.at[which])
    for c in range(PARTS):
        await_bytes(acc.at[pl.ds(PARTS * c, PARTS)], out_sem.at[c])

    @pl.when(row != 3)
    def _():
        await_bytes(fol_pass, pass_send.at[0])

    @pl.when(row != 0)
    def _():
        await_bytes(hand_pass, pass_send.at[1])


def on_device(orbitals, pair_flags, cutoff_reach):
    tall, wide = cas_tables()
    reach = jnp.pad(cutoff_reach.astype(jnp.bfloat16), ((0, N - HALF), (0, N - HALF)))
    block = pltpu.VMEM((PLANES, N, N), jnp.float32)
    planes = pltpu.VMEM((2, PLANES, N, W), jnp.float32)
    lines = pltpu.VMEM((2, N, PLANES, W), jnp.float32)
    dma = pltpu.SemaphoreType.DMA
    vmem = pl.BlockSpec(memory_space=pltpu.VMEM)
    anywhere = pl.BlockSpec(memory_space=pl.ANY)
    return pl.pallas_call(
        kernel,
        out_shape=(
            jax.ShapeDtypeStruct((1, PLANES, N, N), jnp.float32),
            jax.ShapeDtypeStruct((1, 1), jnp.float32),
        ),
        in_specs=[anywhere, pl.BlockSpec(memory_space=pltpu.SMEM), vmem, vmem, vmem],
        out_specs=(anywhere, vmem),
        scratch_shapes=[
            block, block, planes, planes, lines, lines, lines, lines, lines, block, block,
            pltpu.VMEM((8, 128), jnp.float32), pltpu.VMEM((GROUP, 8, 128), jnp.float32),
            pltpu.VMEM((PARTS, N, N), jnp.float32), pltpu.VMEM((2, PARTS * PLANES, PLANES, W), jnp.float32),
            dma((PARTS,)), dma, dma((PARTS,)), dma((2,)), dma((2,)), dma((2,)), dma((2, 2)),
            dma, dma((PARTS,)), dma((PARTS,)), dma, dma, dma((2,)), dma((2,)),
        ],
        compiler_params=pltpu.CompilerParams(
            collective_id=0, has_side_effects=True, vmem_limit_bytes=58 * 2**20
        ),
        name="exchange",
    )(orbitals, pair_flags, reach, jnp.asarray(tall), jnp.asarray(wide))


def solution(mesh):
    return jax.shard_map(
        on_device,
        mesh=mesh,
        in_specs=(P("band", "fft", None, None), P(), P()),
        out_specs=(P("band", "fft", None, None), P("band", None)),
        check_vma=False,
    )
```

```python
import functools
import math

import jax
import jax.numpy as jnp
import ml_dtypes
import numpy as np
from jax import lax
from jax.experimental import pallas as pl
from jax.experimental.pallas import tpu as pltpu
from jax.sharding import PartitionSpec as P

MESH = pl.DeviceIdType.MESH
N = 256
PLANES = 16
HALF = 129
BANDS = 8
GROUP = 16
PARTS = 4
W = 128

FOLLOWING = ((0, 4, 0), (4, 1, 0), (5, 3, 2), (8, 2, 2), (10, 2, None), (12, 4, None))
NF = len(FOLLOWING)
HANDED = (1, 3, 1, None)

STEPS = (
    (2, 1, 0), (1, 0, 0), (3, 0, 1), (0, 1, 0), (2, 0, 0), (1, 1, 1), (3, 1, 0), (0, 1, 1),
    (2, 1, 1), (3, 0, 0), (1, 0, 1), (0, 0, 1), (2, 0, 1), (3, 1, 1), (1, 1, 0),
)


def cas_tables():
    steps = np.arange(N)
    angles = (steps[:, None] * steps[None, :] % N) * (2.0 * math.pi / N)
    table = np.cos(angles) + np.sin(angles)
    terms = []
    for _ in range(3):
        terms.append(table.astype(ml_dtypes.bfloat16))
        table = table - terms[-1].astype(np.float64)
    order = [terms[i] for i in (0, 1, 0, 1, 2, 0)]
    return np.concatenate(order, axis=0), np.concatenate(order, axis=1)


def split(x, axis, passes):
    high = x.astype(jnp.bfloat16)
    rest = x - high.astype(jnp.float32)
    middle = rest.astype(jnp.bfloat16)
    terms = [high, high, middle]
    if passes == 6:
        low = (rest - middle.astype(jnp.float32)).astype(jnp.bfloat16)
        terms = terms + [middle, high, low]
    return jnp.concatenate(terms, axis=axis)


def kernel(
    orb_hbm, flags_hbm, reach_hbm, tall, wide, out, margin,
    flags, reach, padded,
    orb, fol, a0, a1, s0, s1, b0, b1, hin, ktab, part, parts, fol_pass, hand_pass,
    small_sem, load_sem, fol_send, fol_recv, fwd_send, fwd_recv, back_send, back_recv,
    hand_send, hand_recv, sum_send, sum_recv, pass_send, pass_recv,
):
    acc = out.at[0]
    band = lax.axis_index("band")
    me = lax.axis_index("fft")
    row = lax.rem(band, 4)
    across = 4 - 4 * (band // 4)
    after = lax.rem(band + 1, BANDS)
    before = lax.rem(band + BANDS - 1, BANDS)

    def partner(step):
        x, z, core = me // 4, (me // 2) % 2, me % 2
        return ((x + step[0]) % 4) * 4 + ((z + step[1]) % 2) * 2 + (core + step[2]) % 2

    def send(source, target, send_sem, recv_sem, device):
        pltpu.make_async_remote_copy(
            src_ref=source, dst_ref=target, send_sem=send_sem, recv_sem=recv_sem,
            device_id=device, device_id_type=MESH,
        ).start()

    def await_bytes(ref, sem):
        pltpu.make_async_copy(ref, ref, sem).wait()

    def right(x, passes):
        return jnp.dot(split(x, 1, passes), tall[: passes * N], preferred_element_type=jnp.float32)

    def left(x, passes):
        return jnp.dot(wide[:, : passes * N], split(x, 0, passes), preferred_element_type=jnp.float32)

    def put(ref, index, x):
        for h in range(2):
            ref[h, index] = x[:, h * W:(h + 1) * W]

    def line(ref, index):
        halves = [ref.at[h].reshape(N * PLANES, W)[pl.ds(index, N, stride=PLANES), :] for h in range(2)]
        return jnp.concatenate(halves, axis=1)

    loads = [
        pltpu.make_async_copy(
            orb_hbm.at[0, pl.ds(c * PARTS, PARTS)], orb.at[pl.ds(c * PARTS, PARTS)], load_sem.at[c]
        )
        for c in range(PARTS)
    ]
    flags_load = pltpu.make_async_copy(flags_hbm, flags, small_sem.at[0])
    reach_load = pltpu.make_async_copy(reach_hbm, reach, small_sem.at[1])
    for load in (*loads, flags_load, reach_load):
        load.start()

    barrier = pltpu.get_barrier_semaphore()
    for step in STEPS:
        pl.semaphore_signal(barrier, inc=1, device_id=(band, partner(step)), device_id_type=MESH)
    for ahead in range(1, BANDS):
        other = lax.rem(band + ahead, BANDS)
        pl.semaphore_signal(barrier, inc=1, device_id=(other, me), device_id_type=MESH)
    pl.semaphore_wait(barrier, GROUP - 1 + BANDS - 1)

    flags_load.wait()
    own_weight = flags[0, band].astype(jnp.float32)
    next_weight = flags[1, band].astype(jnp.float32)

    for c in range(PARTS):
        loads[c].wait()

    @pl.when(row != 0)
    def _():
        for c in range(PARTS):
            rows = pl.ds(c * PARTS, PARTS)
            send(orb.at[rows], fol.at[rows], fol_send, fol_recv.at[c], (before, me))

    @pl.when(row == 0)
    def _():
        for n, (first, count, via) in enumerate(FOLLOWING):
            rows = pl.ds(first, count)
            if via is None:
                send(orb.at[rows], fol.at[rows], fol_send, fol_recv.at[first // PARTS], (across + 3, me))
            else:
                send(orb.at[rows], fol_pass.at[rows], fol_send, pass_recv.at[n], (across + via, me))

    def pass_following():
        for n, (first, count, via) in enumerate(FOLLOWING):
            if via is None:
                continue

            @pl.when(row == via)
            def _(n=n, rows=pl.ds(first, count), via=via, c=first // PARTS):
                await_bytes(fol_pass.at[rows], pass_recv.at[n])
                send(fol_pass.at[rows], fol.at[rows], pass_send.at[n], fol_recv.at[c], (band - via + 3, me))

    def forward(c, pair, weight, spectrum, lines, which):
        for q in range(PARTS):
            p = c * PARTS + q
            density = weight * orb[p] * pair[p]
            put(spectrum, p, left(right(density, 6), 6))
        rows = pl.ds(c * PARTS, PARTS)
        mine = pl.ds(me * PLANES + c * PARTS, PARTS)
        for step in STEPS:
            g = partner(step)
            send(
                spectrum.at[:, rows, pl.ds(pl.multiple_of(g * PLANES, PLANES), PLANES)],
                lines.at[:, mine], fwd_send.at[which], fwd_recv.at[which], (band, g),
            )
        pltpu.make_async_copy(
            spectrum.at[:, rows, pl.ds(pl.multiple_of(me * PLANES, PLANES), PLANES)],
            lines.at[:, mine], fwd_recv.at[which],
        ).start()

    def own_chunk(c, carry):
        forward(c, orb, own_weight, a0, s0, 0)
        return carry

    lax.fori_loop(0, 2, own_chunk, 0)

    def fold(shape, axis):
        k = lax.broadcasted_iota(jnp.int32, shape, axis)
        return jnp.minimum(k, N - k)

    level = lax.broadcasted_iota(jnp.int32, (N, N), 1)
    pick_x = (fold((N, N), 0) == level).astype(jnp.bfloat16)
    reach_load.wait()
    padded[...] = jnp.zeros_like(padded)
    padded[:HALF, :HALF] = reach[...].astype(jnp.float32)
    limits = padded[...].astype(jnp.bfloat16)
    by_x = jnp.dot(pick_x, limits, preferred_element_type=jnp.float32).astype(jnp.bfloat16)

    def table_step(k, carry):
        ky = me * PLANES + k
        fold_y = jnp.minimum(ky, N - ky)
        pick_y = (lax.broadcasted_iota(jnp.int32, (N, N), 0) == fold_y).astype(jnp.bfloat16)
        limit = jnp.dot(by_x, pick_y, preferred_element_type=jnp.float32)
        fold_x, fold_z = fold((N, N), 0), fold((N, N), 1)
        squares = fold_x * fold_x + fold_z * fold_z + fold_y * fold_y
        kept = (fold_z.astype(jnp.float32) <= limit) & (squares > 0)
        value = (64.0 / N**3) / jnp.maximum(squares, 1).astype(jnp.float32)
        ktab[k] = jnp.where(kept, value, 0.0)
        return carry

    lax.fori_loop(0, PLANES, table_step, 0)

    def cross_chunk(i, carry):
        c = lax.rem(i + 3 * (row // 3), PARTS)
        await_bytes(fol.at[pl.ds(0, PARTS)], fol_recv.at[c])
        forward(c, fol, next_weight, a1, s1, 1)
        return carry

    def middle(lines, restored, which, mixed=None):
        await_bytes(lines, fwd_recv.at[which])
        await_bytes(restored.at[:, pl.ds(0, GROUP - 1)], fwd_send.at[which])

        def one(k):
            put(restored, k, left(left(line(lines, k), 6) * ktab[k], 3))

        def some(i, carry):
            for k in range(PARTS):
                one(PARTS * i + k)
            if mixed is not None:
                send_back(restored, mixed, which, 0, PARTS * i, PARTS)
            return carry

        lax.fori_loop(0, PLANES // PARTS, some, 0)

    def send_back(restored, mixed, which, j, first=0, count=PLANES):
        lines = pl.ds(first, count)
        mine = pl.ds(me * PLANES + first, count)
        half = pl.ds(8 * j, 8)
        for step in STEPS:
            g = partner(step)
            send(
                restored.at[:, lines, pl.ds(pl.multiple_of(g * PLANES + 8 * j, 8), 8)],
                mixed.at[:, mine, half], back_send.at[which], back_recv.at[which, j], (band, g),
            )
        pltpu.make_async_copy(
            restored.at[:, lines, pl.ds(pl.multiple_of(me * PLANES + 8 * j, 8), 8)],
            mixed.at[:, mine, half], back_recv.at[which, j],
        ).start()

    pass_following()
    lax.fori_loop(0, 2, cross_chunk, 0)
    lax.fori_loop(2, 3, own_chunk, 0)
    lax.fori_loop(2, 4, cross_chunk, 0)
    lax.fori_loop(3, 4, own_chunk, 0)
    middle(s1, a1, 1, b1)
    send_back(a1, b1, 1, 1)
    middle(s0, a0, 0)

    def potential(mixed, p):
        return right(left(line(mixed, p), 3), 3)

    def hand(j):
        @pl.when(row != 3)
        def _():
            for c in (2 * j, 2 * j + 1):
                rows = pl.ds(PARTS * PLANES * c, PARTS * PLANES)
                send(s0.at[:, rows], hin.at[:, rows], hand_send, hand_recv.at[c], (after, me))

        @pl.when(row == 3)
        def _():
            for c in (2 * j, 2 * j + 1):
                rows = pl.ds(PARTS * PLANES * c, PARTS * PLANES)
                via = HANDED[c]
                if via is None:
                    send(s0.at[:, rows], hin.at[:, rows], hand_send, hand_recv.at[c], (across, me))
                else:
                    send(s0.at[:, rows], hand_pass.at[:, rows], hand_send, pass_recv.at[NF + c], (across + via, me))

    def pass_handed():
        for c, via in enumerate(HANDED):
            if via is None:
                continue

            @pl.when(row == via)
            def _(c=c, rows=pl.ds(PARTS * PLANES * c, PARTS * PLANES), via=via):
                await_bytes(hand_pass.at[:, rows], pass_recv.at[NF + c])
                send(hand_pass.at[:, rows], hin.at[:, rows], pass_send.at[NF + c], hand_recv.at[c], (band - via, me))

    for j in range(2):
        await_bytes(b1.at[:, :, pl.ds(8 * j, 8)], back_recv.at[1, j])

        def cross_out(i, carry, j=j):
            for q in range(2):
                p = 8 * j + 2 * i + q
                coulomb = potential(b1, p)
                acc[p] = fol[p] * coulomb
                handed = orb[p] * coulomb
                for h in range(2):
                    s0[h, pl.ds(p * PLANES, PLANES)] = handed[:, h * W:(h + 1) * W].reshape(PLANES, PLANES, W)
            return carry

        lax.fori_loop(0, 4, cross_out, 0)
        hand(j)
        send_back(a0, b0, 0, j)

    pass_handed()

    for j in range(2):
        await_bytes(b0.at[:, :, pl.ds(8 * j, 8)], back_recv.at[0, j])

        def own_out(i, carry, j=j):
            for q in range(2):
                p = 8 * j + 2 * i + q
                acc[p] = acc[p] + orb[p] * potential(b0, p)
            return carry

        lax.fori_loop(0, 4, own_out, 0)

    part[...] = jnp.zeros_like(part)
    for c in range(PARTS):
        await_bytes(hin.at[:, pl.ds(0, PARTS * PLANES)], hand_recv.at[c])

        def finish(i, carry, c=c):
            p = PARTS * c + i
            given = [hin[h, pl.ds(p * PLANES, PLANES)].reshape(N, W) for h in range(2)]
            field = -(acc[p] + jnp.concatenate(given, axis=1))
            acc[p] = field
            sums = (orb[p] * field).reshape(N // 8, 8, N).sum(axis=0)
            part[...] += sums[:, :W] + sums[:, W:]
            return carry

        lax.fori_loop(0, PARTS, finish, 0)

    for step in STEPS:
        send(part, parts.at[me], sum_send, sum_recv, (band, partner(step)))
    pltpu.make_async_copy(part, parts.at[me], sum_recv).start()
    await_bytes(parts, sum_recv)
    total = jnp.sum(jnp.sum(parts[...], axis=0), keepdims=True)
    margin[...] = total / float(N * N)

    await_bytes(parts.at[pl.ds(0, GROUP - 1)], sum_send)
    await_bytes(fol, fol_send)
    await_bytes(hin, hand_send)
    for which, restored in enumerate((a0, a1)):
        await_bytes(restored.at[:, pl.ds(0, GROUP - 1)], back_send.at[which])
    for n, (first, count, via) in enumerate(FOLLOWING):
        if via is not None:

            @pl.when(row == via)
            def _(n=n, rows=pl.ds(first, count)):
                await_bytes(fol_pass.at[rows], pass_send.at[n])

    for c, via in enumerate(HANDED):
        if via is not None:

            @pl.when(row == via)
            def _(c=c, rows=pl.ds(PARTS * PLANES * c, PARTS * PLANES)):
                await_bytes(hand_pass.at[:, rows], pass_send.at[NF + c])


def on_device(orbitals, pair_flags, cutoff_reach):
    tall, wide = cas_tables()
    block = pltpu.VMEM((PLANES, N, N), jnp.float32)
    planes = pltpu.VMEM((2, PLANES, N, W), jnp.float32)
    lines = pltpu.VMEM((2, N, PLANES, W), jnp.float32)
    dma = pltpu.SemaphoreType.DMA
    vmem = pl.BlockSpec(memory_space=pltpu.VMEM)
    anywhere = pl.BlockSpec(memory_space=pl.ANY)
    return pl.pallas_call(
        kernel,
        out_shape=(
            pltpu.VMEM((1, PLANES, N, N), jnp.float32),
            jax.ShapeDtypeStruct((1, 1), jnp.float32),
        ),
        in_specs=[anywhere, anywhere, anywhere, vmem, vmem],
        out_specs=(vmem, vmem),
        scratch_shapes=[
            pltpu.SMEM((2, BANDS), jnp.int32), pltpu.VMEM((HALF, HALF), jnp.int32), pltpu.VMEM((N, N), jnp.float32),
            block, block, planes, planes, lines, lines, lines, lines, lines, block,
            pltpu.VMEM((8, 128), jnp.float32), pltpu.VMEM((GROUP, 8, 128), jnp.float32),
            pltpu.VMEM((10, N, N), jnp.float32), lines,
            dma((2,)), dma((PARTS,)), dma, dma((PARTS,)), dma((2,)), dma((2,)), dma((2,)), dma((2, 2)),
            dma, dma((PARTS,)), dma, dma, dma((NF + PARTS,)), dma((NF + PARTS,)),
        ],
        compiler_params=pltpu.CompilerParams(
            collective_id=0, has_side_effects=True, vmem_limit_bytes=54 * 2**20
        ),
        name="exchange",
    )(orbitals, pair_flags.T, cutoff_reach, jnp.asarray(tall), jnp.asarray(wide))


def solution(mesh):
    return jax.shard_map(
        on_device,
        mesh=mesh,
        in_specs=(P("band", "fft", None, None), P(), P()),
        out_specs=(P("band", "fft", None, None), P("band", None)),
        check_vma=False,
    )
```

```python
import functools
import math

import jax
import jax.numpy as jnp
import ml_dtypes
import numpy as np
from jax import lax
from jax.experimental import pallas as pl
from jax.experimental.pallas import tpu as pltpu
from jax.sharding import PartitionSpec as P

MESH = pl.DeviceIdType.MESH
N = 256
PLANES = 16
HALF = 129
BANDS = 8
GROUP = 16
PARTS = 4
W = 128

FOLLOWING = ((0, 4, 0), (4, 1, 0), (5, 3, 2), (8, 2, 2), (10, 2, None), (12, 4, None))
NF = len(FOLLOWING)
HANDED = (1, 3, 1, None)

STEPS = (
    (2, 1, 0), (1, 0, 0), (3, 0, 1), (0, 1, 0), (2, 0, 0), (1, 1, 1), (3, 1, 0), (0, 1, 1),
    (2, 1, 1), (3, 0, 0), (1, 0, 1), (0, 0, 1), (2, 0, 1), (3, 1, 1), (1, 1, 0),
)


def cas_tables():
    steps = np.arange(N)
    angles = (steps[:, None] * steps[None, :] % N) * (2.0 * math.pi / N)
    table = np.cos(angles) + np.sin(angles)
    terms = []
    for _ in range(3):
        terms.append(table.astype(ml_dtypes.bfloat16))
        table = table - terms[-1].astype(np.float64)
    order = [terms[i] for i in (0, 1, 0, 1, 2, 0)]
    return np.concatenate(order, axis=0), np.concatenate(order, axis=1)


def split(x, axis, passes):
    high = x.astype(jnp.bfloat16)
    rest = x - high.astype(jnp.float32)
    middle = rest.astype(jnp.bfloat16)
    terms = [high, high, middle]
    if passes == 6:
        low = (rest - middle.astype(jnp.float32)).astype(jnp.bfloat16)
        terms = terms + [middle, high, low]
    return jnp.concatenate(terms, axis=axis)


def kernel(
    orb_hbm, flags_hbm, reach_hbm, tall, wide, out, margin,
    flags, reach, padded,
    orb, fol, a0, a1, s0, s1, b0, b1, hin, ktab, part, parts, fol_pass, hand_pass,
    small_sem, load_sem, fol_send, fol_recv, fwd_send, fwd_recv, back_send, back_recv,
    hand_send, hand_recv, sum_send, sum_recv, pass_send, pass_recv,
):
    acc = out.at[0]
    band = lax.axis_index("band")
    me = lax.axis_index("fft")
    row = lax.rem(band, 4)
    across = 4 - 4 * (band // 4)
    after = lax.rem(band + 1, BANDS)
    before = lax.rem(band + BANDS - 1, BANDS)

    def partner(step):
        x, z, core = me // 4, (me // 2) % 2, me % 2
        return ((x + step[0]) % 4) * 4 + ((z + step[1]) % 2) * 2 + (core + step[2]) % 2

    def send(source, target, send_sem, recv_sem, device):
        pltpu.make_async_remote_copy(
            src_ref=source, dst_ref=target, send_sem=send_sem, recv_sem=recv_sem,
            device_id=device, device_id_type=MESH,
        ).start()

    def await_bytes(ref, sem):
        pltpu.make_async_copy(ref, ref, sem).wait()

    def right(x, passes):
        return jnp.dot(split(x, 1, passes), tall[: passes * N], preferred_element_type=jnp.float32)

    def left(x, passes):
        return jnp.dot(wide[:, : passes * N], split(x, 0, passes), preferred_element_type=jnp.float32)

    def put(ref, index, x):
        for h in range(2):
            ref[h, index] = x[:, h * W:(h + 1) * W]

    def line(ref, index):
        halves = [ref.at[h].reshape(N * PLANES, W)[pl.ds(index, N, stride=PLANES), :] for h in range(2)]
        return jnp.concatenate(halves, axis=1)

    loads = [
        pltpu.make_async_copy(
            orb_hbm.at[0, pl.ds(c * PARTS, PARTS)], orb.at[pl.ds(c * PARTS, PARTS)], load_sem.at[c]
        )
        for c in range(PARTS)
    ]
    flags_load = pltpu.make_async_copy(flags_hbm, flags, small_sem.at[0])
    reach_load = pltpu.make_async_copy(reach_hbm, reach, small_sem.at[1])
    for load in (*loads, flags_load, reach_load):
        load.start()

    barrier = pltpu.get_barrier_semaphore()
    for step in STEPS:
        pl.semaphore_signal(barrier, inc=1, device_id=(band, partner(step)), device_id_type=MESH)
    for ahead in range(1, BANDS):
        other = lax.rem(band + ahead, BANDS)
        pl.semaphore_signal(barrier, inc=1, device_id=(other, me), device_id_type=MESH)
    pl.semaphore_wait(barrier, GROUP - 1 + BANDS - 1)

    flags_load.wait()
    own_weight = flags[0, band].astype(jnp.float32)
    next_weight = flags[1, band].astype(jnp.float32)

    for c in range(PARTS):
        loads[c].wait()

    @pl.when(row != 0)
    def _():
        for c in range(PARTS):
            rows = pl.ds(c * PARTS, PARTS)
            send(orb.at[rows], fol.at[rows], fol_send, fol_recv.at[c], (before, me))

    @pl.when(row == 0)
    def _():
        for n, (first, count, via) in enumerate(FOLLOWING):
            rows = pl.ds(first, count)
            if via is None:
                send(orb.at[rows], fol.at[rows], fol_send, fol_recv.at[first // PARTS], (across + 3, me))
            else:
                send(orb.at[rows], fol_pass.at[rows], fol_send, pass_recv.at[n], (across + via, me))

    def pass_following():
        for n, (first, count, via) in enumerate(FOLLOWING):
            if via is None:
                continue

            @pl.when(row == via)
            def _(n=n, rows=pl.ds(first, count), via=via, c=first // PARTS):
                await_bytes(fol_pass.at[rows], pass_recv.at[n])
                send(fol_pass.at[rows], fol.at[rows], pass_send.at[n], fol_recv.at[c], (band - via + 3, me))

    def forward(c, pair, weight, spectrum, lines, which):
        for q in range(PARTS):
            p = c * PARTS + q
            density = weight * orb[p] * pair[p]
            put(spectrum, p, left(right(density, 6), 6))
        rows = pl.ds(c * PARTS, PARTS)
        mine = pl.ds(me * PLANES + c * PARTS, PARTS)
        for step in STEPS:
            g = partner(step)
            send(
                spectrum.at[:, rows, pl.ds(pl.multiple_of(g * PLANES, PLANES), PLANES)],
                lines.at[:, mine], fwd_send.at[which], fwd_recv.at[which], (band, g),
            )
        pltpu.make_async_copy(
            spectrum.at[:, rows, pl.ds(pl.multiple_of(me * PLANES, PLANES), PLANES)],
            lines.at[:, mine], fwd_recv.at[which],
        ).start()

    def own_chunk(c, carry):
        forward(c, orb, own_weight, a0, s0, 0)
        return carry

    own_chunk(0, 0)

    def fold(shape, axis):
        k = lax.broadcasted_iota(jnp.int32, shape, axis)
        return jnp.minimum(k, N - k)

    level = lax.broadcasted_iota(jnp.int32, (N, N), 1)
    pick_x = (fold((N, N), 0) == level).astype(jnp.bfloat16)
    reach_load.wait()
    padded[...] = jnp.zeros_like(padded)
    padded[:HALF, :HALF] = reach[...].astype(jnp.float32)
    limits = padded[...].astype(jnp.bfloat16)
    by_x = jnp.dot(pick_x, limits, preferred_element_type=jnp.float32).astype(jnp.bfloat16)

    def table_step(k, carry):
        ky = me * PLANES + k
        fold_y = jnp.minimum(ky, N - ky)
        pick_y = (lax.broadcasted_iota(jnp.int32, (N, N), 0) == fold_y).astype(jnp.bfloat16)
        limit = jnp.dot(by_x, pick_y, preferred_element_type=jnp.float32)
        fold_x, fold_z = fold((N, N), 0), fold((N, N), 1)
        squares = fold_x * fold_x + fold_z * fold_z + fold_y * fold_y
        kept = (fold_z.astype(jnp.float32) <= limit) & (squares > 0)
        value = (64.0 / N**3) / jnp.maximum(squares, 1).astype(jnp.float32)
        ktab[k] = jnp.where(kept, value, 0.0)
        return carry

    lax.fori_loop(0, PLANES, table_step, 0)

    def cross_chunk(i, carry):
        c = lax.rem(i + 3 * (row // 3), PARTS)
        await_bytes(fol.at[pl.ds(0, PARTS)], fol_recv.at[c])
        forward(c, fol, next_weight, a1, s1, 1)
        return carry

    def middle(lines, restored, which, mixed=None):
        await_bytes(lines, fwd_recv.at[which])
        await_bytes(restored.at[:, pl.ds(0, GROUP - 1)], fwd_send.at[which])

        def one(k):
            put(restored, k, left(left(line(lines, k), 6) * ktab[k], 3))

        def some(i, carry):
            for k in range(PARTS):
                one(PARTS * i + k)
            if mixed is not None:
                send_back(restored, mixed, which, 0, PARTS * i, PARTS)
            return carry

        lax.fori_loop(0, PLANES // PARTS, some, 0)

    def send_back(restored, mixed, which, j, first=0, count=PLANES, z=None):
        lines = pl.ds(first, count)
        mine = pl.ds(me * PLANES + first, count)
        half = pl.ds(8 * j, 8)
        for step in STEPS:
            if z is not None and step[1] != z:
                continue
            g = partner(step)
            send(
                restored.at[:, lines, pl.ds(pl.multiple_of(g * PLANES + 8 * j, 8), 8)],
                mixed.at[:, mine, half], back_send.at[which], back_recv.at[which, j], (band, g),
            )
        if z != 1:
            pltpu.make_async_copy(
                restored.at[:, lines, pl.ds(pl.multiple_of(me * PLANES + 8 * j, 8), 8)],
                mixed.at[:, mine, half], back_recv.at[which, j],
            ).start()

    pass_following()

    def alternate(i, carry):
        cross_chunk(i, carry)
        own_chunk(i + 1, carry)
        return carry

    lax.fori_loop(0, 2, alternate, 0)
    lax.fori_loop(2, 4, cross_chunk, 0)
    lax.fori_loop(3, 4, own_chunk, 0)
    middle(s1, a1, 1, b1)
    send_back(a1, b1, 1, 1)
    middle(s0, a0, 0)

    def potential(mixed, p):
        return right(left(line(mixed, p), 3), 3)

    def hand(j):
        @pl.when(row != 3)
        def _():
            for c in (2 * j, 2 * j + 1):
                rows = pl.ds(PARTS * PLANES * c, PARTS * PLANES)
                send(s0.at[:, rows], hin.at[:, rows], hand_send, hand_recv.at[c], (after, me))

        @pl.when(row == 3)
        def _():
            for c in (2 * j, 2 * j + 1):
                rows = pl.ds(PARTS * PLANES * c, PARTS * PLANES)
                via = HANDED[c]
                if via is None:
                    send(s0.at[:, rows], hin.at[:, rows], hand_send, hand_recv.at[c], (across, me))
                else:
                    send(s0.at[:, rows], hand_pass.at[:, rows], hand_send, pass_recv.at[NF + c], (across + via, me))

    def pass_handed(parts):
        for c in parts:
            via = HANDED[c]
            if via is None:
                continue

            @pl.when(row == via)
            def _(c=c, rows=pl.ds(PARTS * PLANES * c, PARTS * PLANES), via=via):
                await_bytes(hand_pass.at[:, rows], pass_recv.at[NF + c])
                send(hand_pass.at[:, rows], hin.at[:, rows], pass_send.at[NF + c], hand_recv.at[c], (band - via, me))

    for j in range(2):
        await_bytes(b1.at[:, :, pl.ds(8 * j, 8)], back_recv.at[1, j])

        def cross_out(i, carry, j=j):
            for q in range(2):
                p = 8 * j + 2 * i + q
                coulomb = potential(b1, p)
                acc[p] = fol[p] * coulomb
                handed = orb[p] * coulomb
                for h in range(2):
                    s0[h, pl.ds(p * PLANES, PLANES)] = handed[:, h * W:(h + 1) * W].reshape(PLANES, PLANES, W)
            return carry

        lax.fori_loop(0, 4, cross_out, 0)
        hand(j)
        send_back(a0, b0, 0, j, z=0)

    pass_handed((0, 1))
    send_back(a0, b0, 0, 0, z=1)
    pass_handed((2, 3))
    send_back(a0, b0, 0, 1, z=1)

    for j in range(2):
        await_bytes(b0.at[:, :, pl.ds(8 * j, 8)], back_recv.at[0, j])

        def own_out(i, carry, j=j):
            for q in range(2):
                p = 8 * j + 2 * i + q
                acc[p] = acc[p] + orb[p] * potential(b0, p)
            return carry

        lax.fori_loop(0, 4, own_out, 0)

    part[...] = jnp.zeros_like(part)
    for c in range(PARTS):
        await_bytes(hin.at[:, pl.ds(0, PARTS * PLANES)], hand_recv.at[c])

        def finish(i, carry, c=c):
            p = PARTS * c + i
            given = [hin[h, pl.ds(p * PLANES, PLANES)].reshape(N, W) for h in range(2)]
            field = -(acc[p] + jnp.concatenate(given, axis=1))
            acc[p] = field
            sums = (orb[p] * field).reshape(N // 8, 8, N).sum(axis=0)
            part[...] += sums[:, :W] + sums[:, W:]
            return carry

        lax.fori_loop(0, PARTS, finish, 0)

    for step in STEPS:
        send(part, parts.at[me], sum_send, sum_recv, (band, partner(step)))
    pltpu.make_async_copy(part, parts.at[me], sum_recv).start()
    await_bytes(parts, sum_recv)
    total = jnp.sum(jnp.sum(parts[...], axis=0), keepdims=True)
    margin[...] = total / float(N * N)

    await_bytes(parts.at[pl.ds(0, GROUP - 1)], sum_send)
    await_bytes(fol, fol_send)
    await_bytes(hin, hand_send)
    for which, restored in enumerate((a0, a1)):
        await_bytes(restored.at[:, pl.ds(0, GROUP - 1)], back_send.at[which])
    for n, (first, count, via) in enumerate(FOLLOWING):
        if via is not None:

            @pl.when(row == via)
            def _(n=n, rows=pl.ds(first, count)):
                await_bytes(fol_pass.at[rows], pass_send.at[n])

    for c, via in enumerate(HANDED):
        if via is not None:

            @pl.when(row == via)
            def _(c=c, rows=pl.ds(PARTS * PLANES * c, PARTS * PLANES)):
                await_bytes(hand_pass.at[:, rows], pass_send.at[NF + c])


def on_device(orbitals, pair_flags, cutoff_reach):
    tall, wide = cas_tables()
    block = pltpu.VMEM((PLANES, N, N), jnp.float32)
    planes = pltpu.VMEM((2, PLANES, N, W), jnp.float32)
    lines = pltpu.VMEM((2, N, PLANES, W), jnp.float32)
    dma = pltpu.SemaphoreType.DMA
    vmem = pl.BlockSpec(memory_space=pltpu.VMEM)
    anywhere = pl.BlockSpec(memory_space=pl.ANY)
    return pl.pallas_call(
        kernel,
        out_shape=(
            pltpu.VMEM((1, PLANES, N, N), jnp.float32),
            jax.ShapeDtypeStruct((1, 1), jnp.float32),
        ),
        in_specs=[anywhere, anywhere, anywhere, vmem, vmem],
        out_specs=(vmem, vmem),
        scratch_shapes=[
            pltpu.SMEM((2, BANDS), jnp.int32), pltpu.VMEM((HALF, HALF), jnp.int32), pltpu.VMEM((N, N), jnp.float32),
            block, block, planes, planes, lines, lines, lines, lines, lines, block,
            pltpu.VMEM((8, 128), jnp.float32), pltpu.VMEM((GROUP, 8, 128), jnp.float32),
            pltpu.VMEM((10, N, N), jnp.float32), lines,
            dma((2,)), dma((PARTS,)), dma, dma((PARTS,)), dma((2,)), dma((2,)), dma((2,)), dma((2, 2)),
            dma, dma((PARTS,)), dma, dma, dma((NF + PARTS,)), dma((NF + PARTS,)),
        ],
        compiler_params=pltpu.CompilerParams(
            collective_id=0, has_side_effects=True, vmem_limit_bytes=54 * 2**20
        ),
        name="exchange",
    )(orbitals, pair_flags.T, cutoff_reach, jnp.asarray(tall), jnp.asarray(wide))


def solution(mesh):
    return jax.shard_map(
        on_device,
        mesh=mesh,
        in_specs=(P("band", "fft", None, None), P(), P()),
        out_specs=(P("band", "fft", None, None), P("band", None)),
        check_vma=False,
    )
```

```python
import functools
import math

import jax
import jax.numpy as jnp
import ml_dtypes
import numpy as np
from jax import lax
from jax.experimental import pallas as pl
from jax.experimental.pallas import tpu as pltpu
from jax.sharding import PartitionSpec as P

MESH = pl.DeviceIdType.MESH
N = 256
PLANES = 16
HALF = 129
BANDS = 8
GROUP = 16
PARTS = 4
W = 128

FOLLOWING = ((0, 4, (0,)), (4, 1, (0,)), (5, 3, (2,)), (8, 2, (2,)), (10, 2, ()), (12, 4, ()))
HANDED = ((0, 4, (1,)), (4, 4, (3,)), (8, 4, (1,)), (12, 4, ()))
NF = len(FOLLOWING)

STEPS = (
    (2, 1, 0), (1, 0, 0), (3, 0, 1), (0, 1, 0), (2, 0, 0), (1, 1, 1), (3, 1, 0), (0, 1, 1),
    (2, 1, 1), (3, 0, 0), (1, 0, 1), (0, 0, 1), (2, 0, 1), (3, 1, 1), (1, 1, 0),
)


def cas_tables():
    steps = np.arange(N)
    angles = (steps[:, None] * steps[None, :] % N) * (2.0 * math.pi / N)
    table = np.cos(angles) + np.sin(angles)
    terms = []
    for _ in range(3):
        terms.append(table.astype(ml_dtypes.bfloat16))
        table = table - terms[-1].astype(np.float64)
    order = [terms[i] for i in (0, 1, 0, 1, 2, 0)]
    return np.concatenate(order, axis=0), np.concatenate(order, axis=1)


def split(x, axis, passes):
    high = x.astype(jnp.bfloat16)
    rest = x - high.astype(jnp.float32)
    middle = rest.astype(jnp.bfloat16)
    terms = [high, high, middle]
    if passes == 6:
        low = (rest - middle.astype(jnp.float32)).astype(jnp.bfloat16)
        terms = terms + [middle, high, low]
    return jnp.concatenate(terms, axis=axis)


def kernel(
    orb_hbm, flags_hbm, reach_hbm, tall, wide, out, margin,
    flags, reach, padded,
    orb, fol, a0, a1, s0, s1, b0, b1, hin, ktab, part, parts, fol_pass, hand_pass,
    small_sem, load_sem, fol_send, fol_recv, fwd_send, fwd_recv, back_send, back_recv,
    hand_send, hand_recv, sum_send, sum_recv, pass_send, pass_recv,
):
    acc = out.at[0]
    band = lax.axis_index("band")
    me = lax.axis_index("fft")
    row = lax.rem(band, 4)
    across = 4 - 4 * (band // 4)
    after = lax.rem(band + 1, BANDS)
    before = lax.rem(band + BANDS - 1, BANDS)

    def partner(step):
        x, z, core = me // 4, (me // 2) % 2, me % 2
        return ((x + step[0]) % 4) * 4 + ((z + step[1]) % 2) * 2 + (core + step[2]) % 2

    def send(source, target, send_sem, recv_sem, device):
        pltpu.make_async_remote_copy(
            src_ref=source, dst_ref=target, send_sem=send_sem, recv_sem=recv_sem,
            device_id=device, device_id_type=MESH,
        ).start()

    def await_bytes(ref, sem):
        pltpu.make_async_copy(ref, ref, sem).wait()

    def right(x, passes):
        return jnp.dot(split(x, 1, passes), tall[: passes * N], preferred_element_type=jnp.float32)

    def left(x, passes):
        return jnp.dot(wide[:, : passes * N], split(x, 0, passes), preferred_element_type=jnp.float32)

    def put(ref, index, x):
        for h in range(2):
            ref[h, index] = x[:, h * W:(h + 1) * W]

    def line(ref, index):
        halves = [ref.at[h].reshape(N * PLANES, W)[pl.ds(index, N, stride=PLANES), :] for h in range(2)]
        return jnp.concatenate(halves, axis=1)

    loads = [
        pltpu.make_async_copy(
            orb_hbm.at[0, pl.ds(c * PARTS, PARTS)], orb.at[pl.ds(c * PARTS, PARTS)], load_sem.at[c]
        )
        for c in range(PARTS)
    ]
    flags_load = pltpu.make_async_copy(flags_hbm, flags, small_sem.at[0])
    reach_load = pltpu.make_async_copy(reach_hbm, reach, small_sem.at[1])
    for load in (*loads, flags_load, reach_load):
        load.start()

    barrier = pltpu.get_barrier_semaphore()
    for step in STEPS:
        pl.semaphore_signal(barrier, inc=1, device_id=(band, partner(step)), device_id_type=MESH)
    for ahead in range(1, BANDS):
        other = lax.rem(band + ahead, BANDS)
        pl.semaphore_signal(barrier, inc=1, device_id=(other, me), device_id_type=MESH)
    pl.semaphore_wait(barrier, GROUP - 1 + BANDS - 1)

    flags_load.wait()
    own_weight = flags[0, band].astype(jnp.float32)
    next_weight = flags[1, band].astype(jnp.float32)

    for c in range(PARTS):
        loads[c].wait()

    @pl.when(row != 0)
    def _():
        for c in range(PARTS):
            rows = pl.ds(c * PARTS, PARTS)
            send(orb.at[rows], fol.at[rows], fol_send, fol_recv.at[c], (before, me))

    @pl.when(row == 0)
    def _():
        for n, (first, count, path) in enumerate(FOLLOWING):
            rows = pl.ds(first, count)
            if path:
                send(orb.at[rows], fol_pass.at[rows], fol_send, pass_recv.at[n], (across + path[0], me))
            else:
                send(orb.at[rows], fol.at[rows], fol_send, fol_recv.at[first // PARTS], (across + 3, me))

    def pass_on(n, held, rows, path, hop, final, arrived, end):
        @pl.when(row == path[hop])
        def _():
            await_bytes(held(rows), pass_recv.at[n])
            base = band - path[hop]
            if hop + 1 < len(path):
                send(held(rows), held(rows), pass_send.at[n], pass_recv.at[n], (base + path[hop + 1], me))
            else:
                send(held(rows), final(rows), pass_send.at[n], arrived, (base + end, me))

    def pass_following(n, hop):
        first, count, path = FOLLOWING[n]
        pass_on(
            n, lambda r: fol_pass.at[r], pl.ds(first, count), path, hop,
            lambda r: fol.at[r], fol_recv.at[first // PARTS], 3,
        )

    def forward(c, pair, weight, spectrum, lines, which):
        def some_planes(i, carry):
            for q in range(2):
                p = c * PARTS + 2 * i + q
                density = weight * orb[p] * pair[p]
                put(spectrum, p, left(right(density, 6), 6))
            return carry

        lax.fori_loop(0, PARTS // 2, some_planes, 0)
        rows = pl.ds(c * PARTS, PARTS)
        mine = pl.ds(me * PLANES + c * PARTS, PARTS)
        for step in STEPS:
            g = partner(step)
            send(
                spectrum.at[:, rows, pl.ds(pl.multiple_of(g * PLANES, PLANES), PLANES)],
                lines.at[:, mine], fwd_send.at[which], fwd_recv.at[which], (band, g),
            )
        pltpu.make_async_copy(
            spectrum.at[:, rows, pl.ds(pl.multiple_of(me * PLANES, PLANES), PLANES)],
            lines.at[:, mine], fwd_recv.at[which],
        ).start()

    def own_chunk(c, carry):
        forward(c, orb, own_weight, a0, s0, 0)
        return carry

    own_chunk(0, 0)

    def fold(shape, axis):
        k = lax.broadcasted_iota(jnp.int32, shape, axis)
        return jnp.minimum(k, N - k)

    level = lax.broadcasted_iota(jnp.int32, (N, N), 1)
    pick_x = (fold((N, N), 0) == level).astype(jnp.bfloat16)
    reach_load.wait()
    padded[...] = jnp.zeros_like(padded)
    padded[:HALF, :HALF] = reach[...].astype(jnp.float32)
    limits = padded[...].astype(jnp.bfloat16)
    by_x = jnp.dot(pick_x, limits, preferred_element_type=jnp.float32).astype(jnp.bfloat16)

    def table_step(k, carry):
        ky = me * PLANES + k
        fold_y = jnp.minimum(ky, N - ky)
        pick_y = (lax.broadcasted_iota(jnp.int32, (N, N), 0) == fold_y).astype(jnp.bfloat16)
        limit = jnp.dot(by_x, pick_y, preferred_element_type=jnp.float32)
        fold_x, fold_z = fold((N, N), 0), fold((N, N), 1)
        squares = fold_x * fold_x + fold_z * fold_z + fold_y * fold_y
        kept = (fold_z.astype(jnp.float32) <= limit) & (squares > 0)
        value = (64.0 / N**3) / jnp.maximum(squares, 1).astype(jnp.float32)
        ktab[k] = jnp.where(kept, value, 0.0)
        return carry

    lax.fori_loop(0, PLANES, table_step, 0)

    def cross_chunk(i, shift):
        c = lax.rem(i + (row // 3) * shift, PARTS)
        await_bytes(fol.at[pl.ds(0, PARTS)], fol_recv.at[c])
        forward(c, fol, next_weight, a1, s1, 1)

    def middle(lines, restored, which, mixed=None):
        await_bytes(lines, fwd_recv.at[which])
        await_bytes(restored.at[:, pl.ds(0, GROUP - 1)], fwd_send.at[which])

        def one(k):
            put(restored, k, left(left(line(lines, k), 6) * ktab[k], 3))

        def some(i, carry):
            def few(n, inner):
                for q in range(2):
                    one(PARTS * i + 2 * n + q)
                return inner

            lax.fori_loop(0, PARTS // 2, few, 0)
            if mixed is not None:
                send_back(restored, mixed, which, 0, PARTS * i, PARTS)
            return carry

        lax.fori_loop(0, PLANES // PARTS, some, 0)

    def send_back(restored, mixed, which, j, first=0, count=PLANES, z=None):
        lines = pl.ds(first, count)
        mine = pl.ds(me * PLANES + first, count)
        half = pl.ds(8 * j, 8)
        for step in STEPS:
            if z is not None and step[1] != z:
                continue
            g = partner(step)
            send(
                restored.at[:, lines, pl.ds(pl.multiple_of(g * PLANES + 8 * j, 8), 8)],
                mixed.at[:, mine, half], back_send.at[which], back_recv.at[which, j], (band, g),
            )
        if z != 1:
            pltpu.make_async_copy(
                restored.at[:, lines, pl.ds(pl.multiple_of(me * PLANES + 8 * j, 8), 8)],
                mixed.at[:, mine, half], back_recv.at[which, j],
            ).start()

    for n in range(4):
        pass_following(n, 0)
    cross_chunk(0, 3)
    own_chunk(1, 0)
    cross_chunk(1, 3)
    early = jnp.where(row == 1, 1, 0)
    lax.fori_loop(2, 3 + early, own_chunk, 0)

    def last_two(i, carry):
        cross_chunk(i, 3)
        return carry

    lax.fori_loop(2, 4, last_two, 0)
    lax.fori_loop(3 + early, 4, own_chunk, 0)
    middle(s1, a1, 1, b1)
    send_back(a1, b1, 1, 1)
    middle(s0, a0, 0)

    def potential(mixed, p):
        return right(left(line(mixed, p), 3), 3)

    def hand(j):
        @pl.when(row != 3)
        def _():
            for c in (2 * j, 2 * j + 1):
                rows = pl.ds(PARTS * PLANES * c, PARTS * PLANES)
                send(s0.at[:, rows], hin.at[:, rows], hand_send, hand_recv.at[c], (after, me))

        @pl.when(row == 3)
        def _():
            for n, (first, count, path) in enumerate(HANDED):
                if first // 8 != j:
                    continue
                rows = pl.ds(PLANES * first, PLANES * count)
                if path:
                    target, arrived, device = hand_pass, pass_recv.at[NF + n], across + path[0]
                else:
                    target, arrived, device = hin, hand_recv.at[first // PARTS], across
                send(s0.at[:, rows], target.at[:, rows], hand_send, arrived, (device, me))

    def pass_handed(n, hop):
        first, count, path = HANDED[n]
        pass_on(
            NF + n, lambda r: hand_pass.at[:, r], pl.ds(PLANES * first, PLANES * count), path, hop,
            lambda r: hin.at[:, r], hand_recv.at[first // PARTS], 0,
        )

    for j in range(2):
        await_bytes(b1.at[:, :, pl.ds(8 * j, 8)], back_recv.at[1, j])

        def cross_out(i, carry, j=j):
            for q in range(2):
                p = 8 * j + 2 * i + q
                coulomb = potential(b1, p)
                acc[p] = fol[p] * coulomb
                handed = orb[p] * coulomb
                for h in range(2):
                    s0[h, pl.ds(p * PLANES, PLANES)] = handed[:, h * W:(h + 1) * W].reshape(PLANES, PLANES, W)
            return carry

        lax.fori_loop(0, 4, cross_out, 0)
        hand(j)
        send_back(a0, b0, 0, j, z=0)

    pass_handed(0, 0)
    pass_handed(1, 0)
    send_back(a0, b0, 0, 0, z=1)
    pass_handed(2, 0)
    send_back(a0, b0, 0, 1, z=1)

    for j in range(2):
        await_bytes(b0.at[:, :, pl.ds(8 * j, 8)], back_recv.at[0, j])

        def own_out(i, carry, j=j):
            for q in range(2):
                p = 8 * j + 2 * i + q
                acc[p] = acc[p] + orb[p] * potential(b0, p)
            return carry

        lax.fori_loop(0, 4, own_out, 0)

    part[...] = jnp.zeros_like(part)
    for c in range(PARTS):
        await_bytes(hin.at[:, pl.ds(0, PARTS * PLANES)], hand_recv.at[c])

        def finish(i, carry, c=c):
            p = PARTS * c + i
            given = [hin[h, pl.ds(p * PLANES, PLANES)].reshape(N, W) for h in range(2)]
            field = -(acc[p] + jnp.concatenate(given, axis=1))
            acc[p] = field
            sums = (orb[p] * field).reshape(N // 8, 8, N).sum(axis=0)
            part[...] += sums[:, :W] + sums[:, W:]
            return carry

        lax.fori_loop(0, PARTS, finish, 0)

    for step in STEPS:
        send(part, parts.at[me], sum_send, sum_recv, (band, partner(step)))
    pltpu.make_async_copy(part, parts.at[me], sum_recv).start()
    await_bytes(parts, sum_recv)
    total = jnp.sum(jnp.sum(parts[...], axis=0), keepdims=True)
    margin[...] = total / float(N * N)

    await_bytes(parts.at[pl.ds(0, GROUP - 1)], sum_send)
    await_bytes(fol, fol_send)
    await_bytes(hin, hand_send)
    for which, restored in enumerate((a0, a1)):
        await_bytes(restored.at[:, pl.ds(0, GROUP - 1)], back_send.at[which])
    for n, (first, count, path) in enumerate(FOLLOWING):
        for at_row in path:

            @pl.when(row == at_row)
            def _(n=n, rows=pl.ds(first, count)):
                await_bytes(fol_pass.at[rows], pass_send.at[n])

    for n, (first, count, path) in enumerate(HANDED):
        for at_row in path:

            @pl.when(row == at_row)
            def _(n=n, rows=pl.ds(PLANES * first, PLANES * count)):
                await_bytes(hand_pass.at[:, rows], pass_send.at[NF + n])


def on_device(orbitals, pair_flags, cutoff_reach):
    tall, wide = cas_tables()
    block = pltpu.VMEM((PLANES, N, N), jnp.float32)
    planes = pltpu.VMEM((2, PLANES, N, W), jnp.float32)
    lines = pltpu.VMEM((2, N, PLANES, W), jnp.float32)
    dma = pltpu.SemaphoreType.DMA
    vmem = pl.BlockSpec(memory_space=pltpu.VMEM)
    anywhere = pl.BlockSpec(memory_space=pl.ANY)
    return pl.pallas_call(
        kernel,
        out_shape=(
            pltpu.VMEM((1, PLANES, N, N), jnp.float32),
            jax.ShapeDtypeStruct((1, 1), jnp.float32),
        ),
        in_specs=[anywhere, anywhere, anywhere, vmem, vmem],
        out_specs=(vmem, vmem),
        scratch_shapes=[
            pltpu.SMEM((2, BANDS), jnp.int32), pltpu.VMEM((HALF, HALF), jnp.int32), pltpu.VMEM((N, N), jnp.float32),
            block, block, planes, planes, lines, lines, lines, lines, lines, block,
            pltpu.VMEM((8, 128), jnp.float32), pltpu.VMEM((GROUP, 8, 128), jnp.float32),
            pltpu.VMEM((12, N, N), jnp.float32), lines,
            dma((2,)), dma((PARTS,)), dma, dma((PARTS,)), dma((2,)), dma((2,)), dma((2,)), dma((2, 2)),
            dma, dma((PARTS,)), dma, dma, dma((NF + len(HANDED),)), dma((NF + len(HANDED),)),
        ],
        compiler_params=pltpu.CompilerParams(
            collective_id=0, has_side_effects=True, vmem_limit_bytes=54 * 2**20
        ),
        name="exchange",
    )(orbitals, pair_flags.T, cutoff_reach, jnp.asarray(tall), jnp.asarray(wide))


def solution(mesh):
    return jax.shard_map(
        on_device,
        mesh=mesh,
        in_specs=(P("band", "fft", None, None), P(), P()),
        out_specs=(P("band", "fft", None, None), P("band", None)),
        check_vma=False,
    )
```

```python
import functools
import math

import jax
import jax.numpy as jnp
import ml_dtypes
import numpy as np
from jax import lax
from jax.experimental import pallas as pl
from jax.experimental.pallas import tpu as pltpu
from jax.sharding import PartitionSpec as P

MESH = pl.DeviceIdType.MESH
N = 256
PLANES = 16
HALF = 129
BANDS = 8
GROUP = 16
PARTS = 4
W = 128

FOLLOWING = ((0, 4, (0,)), (4, 4, (2,)), (8, 2, (2,)), (10, 2, ()), (12, 4, ()))
HANDED = ((0, 4, (1,)), (4, 4, (3,)), (8, 4, (1,)), (12, 4, ()))
NF = len(FOLLOWING)

STEPS = (
    (2, 1, 0), (1, 0, 0), (3, 0, 1), (0, 1, 0), (2, 0, 0), (1, 1, 1), (3, 1, 0), (0, 1, 1),
    (2, 1, 1), (3, 0, 0), (1, 0, 1), (0, 0, 1), (2, 0, 1), (3, 1, 1), (1, 1, 0),
)


def cas_tables():
    steps = np.arange(N)
    angles = (steps[:, None] * steps[None, :] % N) * (2.0 * math.pi / N)
    table = np.cos(angles) + np.sin(angles)
    terms = []
    for _ in range(3):
        terms.append(table.astype(ml_dtypes.bfloat16))
        table = table - terms[-1].astype(np.float64)
    order = [terms[i] for i in (0, 1, 0, 1, 2, 0)]
    return np.concatenate(order, axis=0), np.concatenate(order, axis=1)


def split(x, axis, passes):
    high = x.astype(jnp.bfloat16)
    rest = x - high.astype(jnp.float32)
    middle = rest.astype(jnp.bfloat16)
    terms = [high, high, middle]
    if passes == 6:
        low = (rest - middle.astype(jnp.float32)).astype(jnp.bfloat16)
        terms = terms + [middle, high, low]
    return jnp.concatenate(terms, axis=axis)


def kernel(
    orb_hbm, flags_hbm, reach_hbm, tall, wide, out, margin,
    flags, reach, padded,
    orb, fol, a0, a1, s0, s1, b0, b1, hin, ktab, part, parts, fol_pass, hand_pass,
    small_sem, load_sem, fol_send, fol_recv, fwd_send, fwd_recv, back_send, back_recv,
    hand_send, hand_recv, sum_send, sum_recv, pass_send, pass_recv,
):
    acc = out.at[0]
    band = lax.axis_index("band")
    me = lax.axis_index("fft")
    row = lax.rem(band, 4)
    across = 4 - 4 * (band // 4)
    after = lax.rem(band + 1, BANDS)
    before = lax.rem(band + BANDS - 1, BANDS)

    def partner(step):
        x, z, core = me // 4, (me // 2) % 2, me % 2
        return ((x + step[0]) % 4) * 4 + ((z + step[1]) % 2) * 2 + (core + step[2]) % 2

    def send(source, target, send_sem, recv_sem, device):
        pltpu.make_async_remote_copy(
            src_ref=source, dst_ref=target, send_sem=send_sem, recv_sem=recv_sem,
            device_id=device, device_id_type=MESH,
        ).start()

    def await_bytes(ref, sem):
        pltpu.make_async_copy(ref, ref, sem).wait()

    def right(x, passes):
        return jnp.dot(split(x, 1, passes), tall[: passes * N], preferred_element_type=jnp.float32)

    def left(x, passes):
        return jnp.dot(wide[:, : passes * N], split(x, 0, passes), preferred_element_type=jnp.float32)

    def put(ref, index, x):
        for h in range(2):
            ref[h, index] = x[:, h * W:(h + 1) * W]

    def line(ref, index):
        halves = [ref.at[h].reshape(N * PLANES, W)[pl.ds(index, N, stride=PLANES), :] for h in range(2)]
        return jnp.concatenate(halves, axis=1)

    loads = [
        pltpu.make_async_copy(
            orb_hbm.at[0, pl.ds(c * PARTS, PARTS)], orb.at[pl.ds(c * PARTS, PARTS)], load_sem.at[c]
        )
        for c in range(PARTS)
    ]
    flags_load = pltpu.make_async_copy(flags_hbm, flags, small_sem.at[0])
    reach_load = pltpu.make_async_copy(reach_hbm, reach, small_sem.at[1])
    for load in (*loads, flags_load, reach_load):
        load.start()

    barrier = pltpu.get_barrier_semaphore()
    for step in STEPS:
        pl.semaphore_signal(barrier, inc=1, device_id=(band, partner(step)), device_id_type=MESH)
    for ahead in range(1, BANDS):
        other = lax.rem(band + ahead, BANDS)
        pl.semaphore_signal(barrier, inc=1, device_id=(other, me), device_id_type=MESH)
    pl.semaphore_wait(barrier, GROUP - 1 + BANDS - 1)

    flags_load.wait()
    own_weight = flags[0, band].astype(jnp.float32)
    next_weight = flags[1, band].astype(jnp.float32)

    for c in range(PARTS):
        loads[c].wait()

    @pl.when(row != 0)
    def _():
        for c in range(PARTS):
            rows = pl.ds(c * PARTS, PARTS)
            send(orb.at[rows], fol.at[rows], fol_send, fol_recv.at[c], (before, me))

    @pl.when(row == 0)
    def _():
        for n, (first, count, path) in enumerate(FOLLOWING):
            rows = pl.ds(first, count)
            if path:
                send(orb.at[rows], fol_pass.at[rows], fol_send, pass_recv.at[n], (across + path[0], me))
            else:
                send(orb.at[rows], fol.at[rows], fol_send, fol_recv.at[first // PARTS], (across + 3, me))

    def pass_on(n, held, rows, path, hop, final, arrived, end):
        @pl.when(row == path[hop])
        def _():
            await_bytes(held(rows), pass_recv.at[n])
            base = band - path[hop]
            if hop + 1 < len(path):
                send(held(rows), held(rows), pass_send.at[n], pass_recv.at[n], (base + path[hop + 1], me))
            else:
                send(held(rows), final(rows), pass_send.at[n], arrived, (base + end, me))

    def pass_following(n, hop):
        first, count, path = FOLLOWING[n]
        pass_on(
            n, lambda r: fol_pass.at[r], pl.ds(first, count), path, hop,
            lambda r: fol.at[r], fol_recv.at[first // PARTS], 3,
        )

    def forward(c, pair, weight, spectrum, lines, which):
        def some_planes(i, carry):
            for q in range(2):
                p = c * PARTS + 2 * i + q
                density = weight * orb[p] * pair[p]
                put(spectrum, p, left(right(density, 6), 6))
            return carry

        lax.fori_loop(0, PARTS // 2, some_planes, 0)
        rows = pl.ds(c * PARTS, PARTS)
        mine = pl.ds(me * PLANES + c * PARTS, PARTS)
        for step in STEPS:
            g = partner(step)
            send(
                spectrum.at[:, rows, pl.ds(pl.multiple_of(g * PLANES, PLANES), PLANES)],
                lines.at[:, mine], fwd_send.at[which], fwd_recv.at[which], (band, g),
            )
        pltpu.make_async_copy(
            spectrum.at[:, rows, pl.ds(pl.multiple_of(me * PLANES, PLANES), PLANES)],
            lines.at[:, mine], fwd_recv.at[which],
        ).start()

    def own_chunk(c, carry):
        forward(c, orb, own_weight, a0, s0, 0)
        return carry

    own_chunk(0, 0)

    def fold(shape, axis):
        k = lax.broadcasted_iota(jnp.int32, shape, axis)
        return jnp.minimum(k, N - k)

    level = lax.broadcasted_iota(jnp.int32, (N, N), 1)
    pick_x = (fold((N, N), 0) == level).astype(jnp.bfloat16)
    reach_load.wait()
    padded[...] = jnp.zeros_like(padded)
    padded[:HALF, :HALF] = reach[...].astype(jnp.float32)
    limits = padded[...].astype(jnp.bfloat16)
    by_x = jnp.dot(pick_x, limits, preferred_element_type=jnp.float32).astype(jnp.bfloat16)

    def table_step(k, carry):
        ky = me * PLANES + k
        fold_y = jnp.minimum(ky, N - ky)
        pick_y = (lax.broadcasted_iota(jnp.int32, (N, N), 0) == fold_y).astype(jnp.bfloat16)
        limit = jnp.dot(by_x, pick_y, preferred_element_type=jnp.float32)
        fold_x, fold_z = fold((N, N), 0), fold((N, N), 1)
        squares = fold_x * fold_x + fold_z * fold_z + fold_y * fold_y
        kept = (fold_z.astype(jnp.float32) <= limit) & (squares > 0)
        value = (64.0 / N**3) / jnp.maximum(squares, 1).astype(jnp.float32)
        ktab[k] = jnp.where(kept, value, 0.0)
        return carry

    lax.fori_loop(0, PLANES, table_step, 0)

    def cross_chunk(i, shift):
        c = lax.rem(i + (row // 3) * shift, PARTS)
        await_bytes(fol.at[pl.ds(0, PARTS)], fol_recv.at[c])
        forward(c, fol, next_weight, a1, s1, 1)

    def middle(lines, restored, which, mixed=None):
        await_bytes(lines, fwd_recv.at[which])
        await_bytes(restored.at[:, pl.ds(0, GROUP - 1)], fwd_send.at[which])

        def one(k):
            put(restored, k, left(left(line(lines, k), 6) * ktab[k], 3))

        def some(i, carry):
            def few(n, inner):
                for q in range(2):
                    one(PARTS * i + 2 * n + q)
                return inner

            lax.fori_loop(0, PARTS // 2, few, 0)
            if mixed is not None:
                send_back(restored, mixed, which, 0, PARTS * i, PARTS)
            return carry

        lax.fori_loop(0, PLANES // PARTS, some, 0)

    def send_back(restored, mixed, which, j, first=0, count=PLANES, z=None):
        lines = pl.ds(first, count)
        mine = pl.ds(me * PLANES + first, count)
        half = pl.ds(8 * j, 8)
        for step in STEPS:
            if z is not None and step[1] != z:
                continue
            g = partner(step)
            send(
                restored.at[:, lines, pl.ds(pl.multiple_of(g * PLANES + 8 * j, 8), 8)],
                mixed.at[:, mine, half], back_send.at[which], back_recv.at[which, j], (band, g),
            )
        if z != 1:
            pltpu.make_async_copy(
                restored.at[:, lines, pl.ds(pl.multiple_of(me * PLANES + 8 * j, 8), 8)],
                mixed.at[:, mine, half], back_recv.at[which, j],
            ).start()

    for n in range(3):
        pass_following(n, 0)
    cross_chunk(0, 3)
    own_chunk(1, 0)
    cross_chunk(1, 3)
    early = jnp.where(row == 1, 1, 0)
    lax.fori_loop(2, 3 + early, own_chunk, 0)

    def last_two(i, carry):
        cross_chunk(i, 3)
        return carry

    lax.fori_loop(2, 4, last_two, 0)
    lax.fori_loop(3 + early, 4, own_chunk, 0)
    middle(s1, a1, 1, b1)
    send_back(a1, b1, 1, 1)
    middle(s0, a0, 0)

    def potential(mixed, p):
        return right(left(line(mixed, p), 3), 3)

    def hand(j):
        @pl.when(row != 3)
        def _():
            for c in (2 * j, 2 * j + 1):
                rows = pl.ds(PARTS * PLANES * c, PARTS * PLANES)
                send(s0.at[:, rows], hin.at[:, rows], hand_send, hand_recv.at[c], (after, me))

        @pl.when(row == 3)
        def _():
            for n, (first, count, path) in enumerate(HANDED):
                if first // 8 != j:
                    continue
                rows = pl.ds(PLANES * first, PLANES * count)
                if path:
                    target, arrived, device = hand_pass, pass_recv.at[NF + n], across + path[0]
                else:
                    target, arrived, device = hin, hand_recv.at[first // PARTS], across
                send(s0.at[:, rows], target.at[:, rows], hand_send, arrived, (device, me))

    def pass_handed(n, hop):
        first, count, path = HANDED[n]
        pass_on(
            NF + n, lambda r: hand_pass.at[:, r], pl.ds(PLANES * first, PLANES * count), path, hop,
            lambda r: hin.at[:, r], hand_recv.at[first // PARTS], 0,
        )

    for j in range(2):
        await_bytes(b1.at[:, :, pl.ds(8 * j, 8)], back_recv.at[1, j])

        def cross_out(i, carry, j=j):
            for q in range(2):
                p = 8 * j + 2 * i + q
                coulomb = potential(b1, p)
                acc[p] = fol[p] * coulomb
                handed = orb[p] * coulomb
                for h in range(2):
                    s0[h, pl.ds(p * PLANES, PLANES)] = handed[:, h * W:(h + 1) * W].reshape(PLANES, PLANES, W)
            return carry

        lax.fori_loop(0, 4, cross_out, 0)
        hand(j)
        send_back(a0, b0, 0, j, z=0)

    pass_handed(0, 0)
    pass_handed(1, 0)
    send_back(a0, b0, 0, 0, z=1)
    pass_handed(2, 0)
    send_back(a0, b0, 0, 1, z=1)

    for j in range(2):
        await_bytes(b0.at[:, :, pl.ds(8 * j, 8)], back_recv.at[0, j])

        def own_out(i, carry, j=j):
            for q in range(2):
                p = 8 * j + 2 * i + q
                acc[p] = acc[p] + orb[p] * potential(b0, p)
            return carry

        lax.fori_loop(0, 4, own_out, 0)

    part[...] = jnp.zeros_like(part)
    for c in range(PARTS):
        await_bytes(hin.at[:, pl.ds(0, PARTS * PLANES)], hand_recv.at[c])

        def finish(i, carry, c=c):
            p = PARTS * c + i
            given = [hin[h, pl.ds(p * PLANES, PLANES)].reshape(N, W) for h in range(2)]
            field = -(acc[p] + jnp.concatenate(given, axis=1))
            acc[p] = field
            sums = (orb[p] * field).reshape(N // 8, 8, N).sum(axis=0)
            part[...] += sums[:, :W] + sums[:, W:]
            return carry

        lax.fori_loop(0, PARTS, finish, 0)

    for step in STEPS:
        send(part, parts.at[me], sum_send, sum_recv, (band, partner(step)))
    pltpu.make_async_copy(part, parts.at[me], sum_recv).start()
    await_bytes(parts, sum_recv)
    total = jnp.sum(jnp.sum(parts[...], axis=0), keepdims=True)
    margin[...] = total / float(N * N)

    await_bytes(parts.at[pl.ds(0, GROUP - 1)], sum_send)
    await_bytes(fol, fol_send)
    await_bytes(hin, hand_send)
    for which, restored in enumerate((a0, a1)):
        await_bytes(restored.at[:, pl.ds(0, GROUP - 1)], back_send.at[which])
    for n, (first, count, path) in enumerate(FOLLOWING):
        for at_row in path:

            @pl.when(row == at_row)
            def _(n=n, rows=pl.ds(first, count)):
                await_bytes(fol_pass.at[rows], pass_send.at[n])

    for n, (first, count, path) in enumerate(HANDED):
        for at_row in path:

            @pl.when(row == at_row)
            def _(n=n, rows=pl.ds(PLANES * first, PLANES * count)):
                await_bytes(hand_pass.at[:, rows], pass_send.at[NF + n])


def on_device(orbitals, pair_flags, cutoff_reach):
    tall, wide = cas_tables()
    block = pltpu.VMEM((PLANES, N, N), jnp.float32)
    planes = pltpu.VMEM((2, PLANES, N, W), jnp.float32)
    lines = pltpu.VMEM((2, N, PLANES, W), jnp.float32)
    dma = pltpu.SemaphoreType.DMA
    vmem = pl.BlockSpec(memory_space=pltpu.VMEM)
    anywhere = pl.BlockSpec(memory_space=pl.ANY)
    return pl.pallas_call(
        kernel,
        out_shape=(
            pltpu.VMEM((1, PLANES, N, N), jnp.float32),
            jax.ShapeDtypeStruct((1, 1), jnp.float32),
        ),
        in_specs=[anywhere, anywhere, anywhere, vmem, vmem],
        out_specs=(vmem, vmem),
        scratch_shapes=[
            pltpu.SMEM((2, BANDS), jnp.int32), pltpu.VMEM((HALF, HALF), jnp.int32), pltpu.VMEM((N, N), jnp.float32),
            block, block, planes, planes, lines, lines, lines, lines, lines, block,
            pltpu.VMEM((8, 128), jnp.float32), pltpu.VMEM((GROUP, 8, 128), jnp.float32),
            pltpu.VMEM((12, N, N), jnp.float32), lines,
            dma((2,)), dma((PARTS,)), dma, dma((PARTS,)), dma((2,)), dma((2,)), dma((2,)), dma((2, 2)),
            dma, dma((PARTS,)), dma, dma, dma((NF + len(HANDED),)), dma((NF + len(HANDED),)),
        ],
        compiler_params=pltpu.CompilerParams(
            collective_id=0, has_side_effects=True, vmem_limit_bytes=54 * 2**20
        ),
        name="exchange",
    )(orbitals, pair_flags.T, cutoff_reach, jnp.asarray(tall), jnp.asarray(wide))


def solution(mesh):
    return jax.shard_map(
        on_device,
        mesh=mesh,
        in_specs=(P("band", "fft", None, None), P(), P()),
        out_specs=(P("band", "fft", None, None), P("band", None)),
        check_vma=False,
    )
```
